256 devices in a mesh: snap: 8 (over x, y_hi), coef: 32 (over y_lo, z, core).
Axes of the slice: x: 4, y: 4 (y_hi: 2, y_lo: 2; y = y_hi * 2 + y_lo), z: 8, core: 2. Of those that a mesh axis runs over, the one named last changes fastest.
Arguments:
- queries: bfloat16 [1024, 65536], P('snap', 'coef'), may hold values from -32 to 32
- slab: bfloat16 [16384, 65536], P('snap', 'coef'), may hold values from -32 to 32
- degree: int32 [65536], P('coef'), may hold values from 0 to 255
- degree_weight: float32 [256], replicated, may hold values from 0.05 to 20
- spread: float32 [1], replicated, may hold values from 1048576 to 3145728
Outputs:
- kernel: float32 [1024, 16384], P('coef', 'snap')
The draws below stay inside these ranges and needn't reach their ends.
All inputs are finite; a program needn't handle non-finite values.
Results may differ from the reference program's by a relative error of at most 0.0003.
Values may be sent and summed in bfloat16 or wider, within the bound.
No kernel may reach another device: no remote copies, remote signals or barrier semaphores. Data moves between devices by JAX's collectives and lax.ppermute only.
A program may use at most 64 MiB of HBM per device.

```python
import math
import jax
import jax.numpy as jnp
from jax import lax

COEFS = 65536
DEGREES = 256
S_DEV = 2048
Q_DEV = 128
QUERIES = 1024
SNAPSHOTS = 16384
N_SNAP = 8


def common_part(key):
    return jax.random.normal(key, (COEFS,), jnp.float32)


def snapshot_panel(key, common, count, ramp_base):
    level_key, noise_key = jax.random.split(key)
    level = jax.random.uniform(level_key, (count, 1), jnp.float32, -1.5, 1.5)
    noise = jax.random.normal(noise_key, (count, COEFS), jnp.float32)
    ramp = jnp.sqrt(ramp_base ** (jnp.arange(COEFS, dtype=jnp.float32) / COEFS))
    return jnp.clip((level * common[None, :] + noise) * ramp[None, :], -32.0, 32.0)


def draw_queries(key, part):
    common = common_part(key)
    key = jax.random.fold_in(key, 11)
    ramp_base = 3.0
    return snapshot_panel(key, common, QUERIES, ramp_base).astype(jnp.bfloat16)


def draw_slab(key, part):
    common = common_part(key)
    key = jax.random.fold_in(key, 23)
    ramp_base = 3.0
    return snapshot_panel(key, common, SNAPSHOTS, ramp_base).astype(jnp.bfloat16)


def touch_ends(entries, key, least, top_value):
    place = [jax.random.randint(jax.random.fold_in(key, axis), (), 0, length) for axis, length in enumerate(entries.shape)]
    longest = entries.shape.index(max(entries.shape))
    next_to = place[:longest] + [(place[longest] + 1) % entries.shape[longest]] + place[longest + 1:]
    return entries.at[tuple(place)].set(least).at[tuple(next_to)].set(top_value)


def setup_inputs(seed: int = 0) -> dict:
    seeds = jax.random.split(jax.random.key(seed), 6)
    queries = draw_queries(jax.random.fold_in(seeds[5], 71), 0)
    slab = draw_slab(jax.random.fold_in(seeds[5], 71), 0)
    degree = touch_ends(jax.random.randint(seeds[2], (COEFS,), 0, DEGREES), jax.random.fold_in(seeds[2], 1), 0, DEGREES - 1).astype(jnp.int32)
    degree_weight = jnp.clip(jnp.exp(jax.random.uniform(seeds[3], (DEGREES,), jnp.float32, math.log(0.05), math.log(20.0))), 0.05, 20.0)
    spread = jnp.clip(jnp.exp(jax.random.uniform(seeds[4], (1,), jnp.float32, math.log(1048576), math.log(3145728))), 1048576, 3145728)
    return {"queries": queries, "slab": slab, "degree": degree, "degree_weight": degree_weight, "spread": spread}


def reference(queries, slab, degree, degree_weight, spread):
    weight_of = degree_weight[degree]
    query_wide = queries.astype(jnp.float32)
    query_norm = jnp.sum(query_wide * query_wide * weight_of[None, :], axis=1)

    def per_block(slab_rows):
        rows_wide = slab_rows.astype(jnp.float32)
        norm_part = jnp.sum(rows_wide * rows_wide * weight_of[None, :], axis=1)
        weighted = (rows_wide * weight_of[None, :]).astype(jnp.bfloat16)
        gram_part = lax.dot_general(queries, weighted, (((1,), (1,)), ((), ())), preferred_element_type=jnp.float32)
        return norm_part, gram_part

    norm_blocks, gram_blocks = lax.map(per_block, slab.reshape(N_SNAP, S_DEV, COEFS))
    slab_norm = norm_blocks.reshape(N_SNAP * S_DEV)
    gram = jnp.transpose(gram_blocks, (1, 0, 2)).reshape(Q_DEV * N_SNAP, N_SNAP * S_DEV)
    distance = query_norm[:, None] + slab_norm[None, :] - 2.0 * gram
    return jnp.exp(-distance / spread[0])
```

```python
import jax
import jax.numpy as jnp
from jax import lax
from jax.sharding import Mesh, PartitionSpec as P

X, YH, YL, Z, CORE = 4, 2, 2, 8, 2
SCALE = 2.0 ** -17
COEF = ("yl", "z", "core")
SNAP = ("x", "yh")


def shift(value, axis, by):
    size = {"x": X, "yh": YH, "yl": YL, "z": Z, "core": CORE}[axis]
    return lax.ppermute(value, axis, [(i, (i + by) % size) for i in range(size)])


def gather_queries(own):
    x, yh = lax.axis_index("x"), lax.axis_index("yh")
    pair = shift(own, "yh", 1)
    left, right, far = shift(own, "x", 1), shift(own, "x", -1), shift(own, "x", 2)
    pair_left, pair_right, pair_far = shift(pair, "x", 1), shift(pair, "x", -1), shift(far, "yh", 1)
    rows = own.shape[0]
    out = jnp.zeros((rows * X * YH, own.shape[1]), own.dtype)
    for block, dx, dy in (
        (own, 0, 0), (pair, 0, 1), (left, -1, 0), (right, 1, 0), (far, 2, 0),
        (pair_left, -1, 1), (pair_right, 1, 1), (pair_far, 2, 1),
    ):
        source = ((x + dx + X) % X) * YH + (yh + dy) % YH
        out = lax.dynamic_update_slice(out, block, (source * rows, 0))
    return out


def pack(value):
    return (value * SCALE).astype(jnp.float16)


def unpack(value):
    return value.astype(jnp.float32) * (1.0 / SCALE)


def reduce_z(held):
    z = lax.axis_index("z")

    def dest(k):
        return lax.dynamic_index_in_dim(held, (z + k + Z) % Z, 1, keepdims=False)

    minus = shift(pack(jnp.stack([dest(-1), dest(-3)])), "z", -1)
    plus = shift(pack(jnp.stack([dest(1), dest(3)])), "z", 1)
    across = dest(4)
    minus2 = shift(pack(across[0]), "z", -2)
    plus2 = shift(pack(across[1]), "z", 2)
    sum_minus = dest(-2) + unpack(minus[1])
    sum_minus = jnp.stack([sum_minus[0] + unpack(minus2), sum_minus[1]])
    sum_plus = dest(2) + unpack(plus[1])
    sum_plus = jnp.stack([sum_plus[0], sum_plus[1] + unpack(plus2)])
    last_minus = shift(pack(sum_minus), "z", -2)
    last_plus = shift(pack(sum_plus), "z", 2)
    return dest(0) + unpack(minus[0]) + unpack(plus[0]) + unpack(last_minus) + unpack(last_plus)


def body(queries, slab, degree, degree_weight, spread):
    levels = jnp.arange(degree_weight.shape[0], dtype=jnp.int32)
    one_hot_table = (degree[:, None] == levels[None, :]).astype(jnp.float32)
    weight_of = jnp.dot(one_hot_table, degree_weight, precision=lax.Precision.HIGHEST)
    slab_wide = slab.astype(jnp.float32)
    weighted_slab = (slab_wide * weight_of[None, :]).astype(jnp.bfloat16)
    slab_part = jnp.sum(slab_wide * slab_wide * weight_of[None, :], axis=1)
    every = gather_queries(queries)
    query_wide = every.astype(jnp.float32)
    query_part = jnp.sum(query_wide * query_wide * weight_of[None, :], axis=1)
    gram_part = lax.dot_general(
        every, weighted_slab, (((1,), (1,)), ((), ())), preferred_element_type=jnp.float32
    )
    partial = query_part[:, None] + slab_part[None, :] - 2.0 * gram_part
    columns = partial.shape[1]
    partial = partial.reshape(YL, Z, CORE, -1, columns)
    core = lax.axis_index("core")
    mine = lax.dynamic_index_in_dim(partial, core, 2, keepdims=False)
    other = lax.dynamic_index_in_dim(partial, 1 - core, 2, keepdims=False)
    held = mine + shift(other, "core", 1)
    summed = reduce_z(held)
    yl = lax.axis_index("yl")
    mine = lax.dynamic_index_in_dim(summed, yl, 0, keepdims=False)
    other = lax.dynamic_index_in_dim(summed, 1 - yl, 0, keepdims=False)
    distance = mine + shift(other, "yl", 1)
    return jnp.exp(-distance / spread[0])


def solution(mesh):
    fine = Mesh(mesh.devices.reshape(X, YH, YL, Z, CORE), ("x", "yh", "yl", "z", "core"))
    placed = (P(SNAP, COEF), P(SNAP, COEF), P(COEF), P(), P())
    return jax.shard_map(
        body, mesh=fine, in_specs=placed, out_specs=P(COEF, SNAP), check_vma=False
    )
```

```python
import functools

import jax
import jax.numpy as jnp
from jax import lax
from jax.experimental import pallas as pl
from jax.experimental.pallas import tpu as pltpu
from jax.sharding import Mesh, PartitionSpec as P

X, YH, YL, Z, CORE = 4, 2, 2, 8, 2
SCALE = 2.0 ** -17
COEF = ("yl", "z", "core")
SNAP = ("x", "yh")
GROUP = 32
CUT = GROUP // 2
KEPT = 2 * GROUP
EARLY = ((0, 0), (0, 1), (-1, 0), (1, 0))
LATE = ((2, 0), (2, 1), (-1, 1), (1, 1))
TILE = 256
VMEM = pl.BlockSpec(memory_space=pltpu.VMEM)
SMEM = pl.BlockSpec(memory_space=pltpu.SMEM)


def shift(value, axis, by):
    size = {"x": X, "yh": YH, "yl": YL, "z": Z, "core": CORE}[axis]
    return lax.ppermute(value, axis, [(i, (i + by) % size) for i in range(size)])


def pack(value):
    return (value * SCALE).astype(jnp.float16)


def unpack(value):
    return value.astype(jnp.float32) * (1.0 / SCALE)


def params(mib):
    return pltpu.CompilerParams(vmem_limit_bytes=mib * 2**20)


def cost(flops, moved):
    return pl.CostEstimate(flops=flops, bytes_accessed=moved, transcendentals=0)


def prepare_kernel(weight, slab, weighted, norm):
    wide = slab[...].astype(jnp.float32)
    scaled = wide * weight[...]
    weighted[...] = scaled.astype(jnp.bfloat16)
    total = jnp.sum(scaled * wide, axis=1, keepdims=True)
    norm[...] = jnp.transpose(jnp.broadcast_to(total, (total.shape[0], 128)))[0:1, :]


def prepare(weight, slab):
    rows, depth = slab.shape
    return pl.pallas_call(
        prepare_kernel,
        grid=(rows // TILE,),
        in_specs=[
            pl.BlockSpec((1, depth), lambda i: (0, 0)),
            pl.BlockSpec((TILE, depth), lambda i: (i, 0)),
        ],
        out_specs=[
            pl.BlockSpec((TILE, depth), lambda i: (i, 0)),
            pl.BlockSpec((1, TILE), lambda i: (0, i)),
        ],
        out_shape=[
            jax.ShapeDtypeStruct((rows, depth), jnp.bfloat16),
            jax.ShapeDtypeStruct((1, rows), jnp.float32),
        ],
        compiler_params=params(12),
        cost_estimate=cost(0, 2**20),
        name="prepare",
    )(weight, slab)


def row_offset(place, offset, low):
    source_x = lax.rem(place[0] + offset[0] + X, X)
    source_yh = lax.rem(place[1] + offset[1], YH)
    yl_from_here = lax.rem(source_x // 2 + place[2], YL)
    z_to = lax.rem(source_x, 2) * 4 + source_yh * 2 + low
    z_from_here = lax.rem(z_to - place[3] + Z, Z)
    return pl.multiple_of((yl_from_here * Z + z_from_here) * GROUP, GROUP)


def early_kernel(offsets, place, weight, slab_norm, slab, *refs):
    count = len(offsets)
    blocks, (other, held, rows, norms) = refs[:count], refs[count:]
    for half in range(CORE):
        for i, block in enumerate(blocks):
            at = pl.ds((half * count + i) * KEPT, KEPT)
            piece = block[half * KEPT : (half + 1) * KEPT, :]
            rows[at, :] = piece
            wide = piece.astype(jnp.float32)
            norms[at, :] = jnp.sum(wide * wide * weight[...], axis=1, keepdims=True)

    @pl.loop(0, slab.shape[0] // TILE)
    def _(n):
        at = pl.ds(pl.multiple_of(n * TILE, TILE), TILE)
        gram = lax.dot_general(
            rows[...], slab[at, :], (((1,), (1,)), ((), ())), preferred_element_type=jnp.float32
        )
        value = norms[...] + slab_norm[:, at] - 2.0 * gram
        other[:, at] = value[: count * KEPT]
        for i, offset in enumerate(offsets):
            for low in range(2):
                start = (count + i) * KEPT + low * GROUP
                held[pl.ds(row_offset(place, offset, low), GROUP), at] = value[start : start + GROUP]


def early_partial(offsets, place, weight, slab_norm, slab, blocks, estimate):
    columns, depth = slab.shape
    kept = len(offsets) * KEPT
    arguments = [place, weight, slab_norm, slab, *blocks]
    return pl.pallas_call(
        functools.partial(early_kernel, offsets),
        in_specs=[SMEM] + [VMEM] * (len(arguments) - 1),
        out_specs=[VMEM, VMEM],
        out_shape=[
            jax.ShapeDtypeStruct((kept, columns), jnp.float32),
            jax.ShapeDtypeStruct((YL * Z * GROUP, columns), jnp.float32),
        ],
        scratch_shapes=[
            pltpu.VMEM((kept * CORE, depth), jnp.bfloat16),
            pltpu.VMEM((kept * CORE, 1), jnp.float32),
        ],
        compiler_params=params(24),
        cost_estimate=estimate,
        name="early_partial",
    )(*arguments)


def add_kernel(offsets, count, place, *refs):
    parts, more, (held, out) = refs[:count], refs[count:-2], refs[-2:]
    for i, offset in enumerate(offsets):
        for low in range(2):
            start = (i * 2 + low) * GROUP
            at = pl.ds(row_offset(place, offset, low), GROUP)
            total = more[0][start : start + GROUP, :] if more else held[at, :]
            part, start = (parts[0], start) if count == 1 else (parts[i], low * GROUP)
            out[at, :] = total + part[start : start + GROUP, :]


def add_into(offsets, place, parts, mine, held, estimate):
    more = [] if mine is None else [mine]
    count = len(parts) + len(more)
    return pl.pallas_call(
        functools.partial(add_kernel, offsets, len(parts)),
        in_specs=[SMEM] + [VMEM] * (count + 1),
        out_specs=VMEM,
        out_shape=jax.ShapeDtypeStruct(held.shape, held.dtype),
        input_output_aliases={count + 1: 0},
        compiler_params=params(16),
        cost_estimate=estimate,
        name="add_into",
    )(place, *parts, *more, held)


def body(queries, slab, degree, degree_weight, spread):
    x, yh, yl, z, core = (lax.axis_index(a) for a in ("x", "yh", "yl", "z", "core"))
    columns, depth = slab.shape

    own = queries.reshape(2, CORE, GROUP, depth)
    own = jnp.concatenate(
        [lax.dynamic_index_in_dim(own, c, 1, keepdims=False).reshape(-1, depth) for c in (1 - core, core)]
    )
    pair = shift(own, "yh", 1)
    far = shift(own, "x", 2)
    left, right = shift(own, "x", 1), shift(own, "x", -1)

    levels = jnp.arange(degree_weight.shape[0], dtype=jnp.int32)
    one_hot_table = (degree[:, None] == levels[None, :]).astype(jnp.float32)
    weight_of = jnp.dot(one_hot_table, degree_weight, precision=lax.Precision.HIGHEST)[None, :]
    weighted_slab, slab_norm = prepare(weight_of, slab)

    pair_left, pair_right = shift(pair, "x", 1), shift(pair, "x", -1)
    pair_far = shift(far, "yh", 1)

    place = jnp.stack([x, yh, yl, z]).astype(jnp.int32)
    small = cost(0, 2**16)
    early_other, held = early_partial(
        EARLY, place, weight_of, slab_norm, weighted_slab, [own, pair, left, right], cost(3 * 10**10, 2**16)
    )
    pieces = [shift(early_other, "core", 1)]
    held = add_into(EARLY, place, pieces, None, held, small)

    def partial(blocks):
        rows = jnp.concatenate(blocks)
        wide = rows.astype(jnp.float32)
        norm = jnp.sum(wide * wide * weight_of, axis=1)
        gram = lax.dot_general(
            rows, weighted_slab, (((1,), (1,)), ((), ())), preferred_element_type=jnp.float32
        )
        return norm[:, None] + slab_norm - 2.0 * gram

    late = lax.optimization_barrier((far, pair_far, pair_left, pair_right, early_other))[:4]
    late_other = shift(partial([b[:KEPT] for b in late]), "core", 1)
    late_mine = partial([b[KEPT:] for b in late])
    held = add_into(LATE, place, [late_other], late_mine, held, small)

    held = held.reshape(YL, Z, GROUP, columns)

    def second(k):
        return held[:, k % Z, CUT:]

    across = shift(pack(held[1, :, :CUT]), "yl", 1)
    minus = shift(pack(jnp.stack([second(-1), second(-3)])), "z", -1)
    plus = shift(pack(jnp.stack([second(1), second(3)])), "z", 1)
    opposite = shift(pack(second(4)), "z", -2)

    def first(k):
        return held[0, k % Z, :CUT] + unpack(across[k % Z])

    minus_first = shift(pack(jnp.stack([first(-1), first(-3)])), "z", -1)
    plus_first = shift(pack(jnp.stack([first(1), first(3)])), "z", 1)
    sum_minus = second(-2) + unpack(minus[1]) + unpack(opposite)
    sum_plus = second(2) + unpack(plus[1])
    last_minus = shift(pack(sum_minus), "z", -2)
    last_plus = shift(jnp.concatenate([pack(sum_plus), pack(first(4))[None]]), "z", 2)

    second_sum = second(0) + unpack(minus[0]) + unpack(plus[0]) + unpack(last_minus) + unpack(last_plus[:2])
    second_sum = second_sum[0] + shift(second_sum[1], "yl", 1)

    first_minus = first(-2) + unpack(minus_first[1])
    first_plus = first(2) + unpack(plus_first[1]) + unpack(last_plus[2])
    end_minus = shift(pack(first_minus), "z", -2)
    end_plus = shift(pack(first_plus), "z", 2)
    first_sum = first(0) + unpack(minus_first[0]) + unpack(plus_first[0]) + unpack(end_minus) + unpack(end_plus)

    distance = jnp.concatenate([first_sum, second_sum], axis=0)
    return jnp.exp(-distance / spread[0])


def solution(mesh):
    fine = Mesh(mesh.devices.reshape(X, YH, YL, Z, CORE), ("x", "yh", "yl", "z", "core"))
    placed = (P(SNAP, COEF), P(SNAP, COEF), P(COEF), P(), P())
    return jax.shard_map(
        body, mesh=fine, in_specs=placed, out_specs=P(COEF, SNAP), check_vma=False
    )
```

```python
import functools

import jax
import jax.numpy as jnp
from jax import lax
from jax.experimental import pallas as pl
from jax.experimental.pallas import tpu as pltpu
from jax.sharding import Mesh, PartitionSpec as P

X, YH, YL, Z, CORE = 4, 2, 2, 8, 2
SCALE = 2.0 ** -17
COEF = ("yl", "z", "core")
SNAP = ("x", "yh")
GROUP = 32
CUT = GROUP // 2
KEPT = 2 * GROUP
EARLY = ((0, 0), (0, 1), (-1, 0), (1, 0), (2, 0))
LATE = ((2, 1), (-1, 1), (1, 1))
TILE = 256
VMEM = pl.BlockSpec(memory_space=pltpu.VMEM)
SMEM = pl.BlockSpec(memory_space=pltpu.SMEM)


def shift(value, axis, by):
    size = {"x": X, "yh": YH, "yl": YL, "z": Z, "core": CORE}[axis]
    return lax.ppermute(value, axis, [(i, (i + by) % size) for i in range(size)])


def pack(value):
    return (value * SCALE).astype(jnp.float16)


def unpack(value):
    return value.astype(jnp.float32) * (1.0 / SCALE)


def params(mib):
    return pltpu.CompilerParams(vmem_limit_bytes=mib * 2**20)


def cost(flops, moved):
    return pl.CostEstimate(flops=flops, bytes_accessed=moved, transcendentals=0)


def prepare_kernel(weight, slab, weighted, norm):
    wide = slab[...].astype(jnp.float32)
    scaled = wide * weight[...]
    weighted[...] = scaled.astype(jnp.bfloat16)
    total = jnp.sum(scaled * wide, axis=1, keepdims=True)
    norm[...] = jnp.transpose(jnp.broadcast_to(total, (total.shape[0], 128)))[0:1, :]


def prepare(weight, slab):
    rows, depth = slab.shape
    return pl.pallas_call(
        prepare_kernel,
        grid=(rows // TILE,),
        in_specs=[
            pl.BlockSpec((1, depth), lambda i: (0, 0)),
            pl.BlockSpec((TILE, depth), lambda i: (i, 0)),
        ],
        out_specs=[
            pl.BlockSpec((TILE, depth), lambda i: (i, 0)),
            pl.BlockSpec((1, TILE), lambda i: (0, i)),
        ],
        out_shape=[
            jax.ShapeDtypeStruct((rows, depth), jnp.bfloat16),
            jax.ShapeDtypeStruct((1, rows), jnp.float32),
        ],
        compiler_params=params(12),
        cost_estimate=cost(0, 2**20),
        name="prepare",
    )(weight, slab)


def row_offset(place, offset, low):
    source_x = lax.rem(place[0] + offset[0] + X, X)
    source_yh = lax.rem(place[1] + offset[1], YH)
    yl_from_here = lax.rem(source_x // 2 + place[2], YL)
    z_to = lax.rem(source_x, 2) * 4 + source_yh * 2 + low
    z_from_here = lax.rem(z_to - place[3] + Z, Z)
    return pl.multiple_of((yl_from_here * Z + z_from_here) * GROUP, GROUP)


def early_kernel(offsets, place, weight, slab_norm, slab, *refs):
    count = len(offsets)
    blocks, (other, held, rows, norms) = refs[:-4], refs[-4:]
    blocks = (blocks[:count], blocks[count:])
    for half in range(CORE):
        for i, block in enumerate(blocks[half]):
            at = pl.ds((half * count + i) * KEPT, KEPT)
            piece = block[...]
            rows[at, :] = piece
            wide = piece.astype(jnp.float32)
            norms[at, :] = jnp.sum(wide * wide * weight[...], axis=1, keepdims=True)

    @pl.loop(0, slab.shape[0] // TILE)
    def _(n):
        at = pl.ds(pl.multiple_of(n * TILE, TILE), TILE)
        gram = lax.dot_general(
            rows[...], slab[at, :], (((1,), (1,)), ((), ())), preferred_element_type=jnp.float32
        )
        value = norms[...] + slab_norm[:, at] - 2.0 * gram
        other[:, at] = value[: count * KEPT]
        for i, offset in enumerate(offsets):
            for low in range(2):
                start = (count + i) * KEPT + low * GROUP
                held[pl.ds(row_offset(place, offset, low), GROUP), at] = value[start : start + GROUP]


def early_partial(offsets, place, weight, slab_norm, slab, blocks, estimate):
    columns, depth = slab.shape
    kept = len(offsets) * KEPT
    arguments = [place, weight, slab_norm, slab, *blocks]
    return pl.pallas_call(
        functools.partial(early_kernel, offsets),
        in_specs=[SMEM] + [VMEM] * (len(arguments) - 1),
        out_specs=[VMEM, VMEM],
        out_shape=[
            jax.ShapeDtypeStruct((kept, columns), jnp.float32),
            jax.ShapeDtypeStruct((YL * Z * GROUP, columns), jnp.float32),
        ],
        scratch_shapes=[
            pltpu.VMEM((kept * CORE, depth), jnp.bfloat16),
            pltpu.VMEM((kept * CORE, 1), jnp.float32),
        ],
        compiler_params=params(24),
        cost_estimate=estimate,
        name="early_partial",
    )(*arguments)


def add_kernel(offsets, count, place, *refs):
    parts, more, (held, out) = refs[:count], refs[count:-2], refs[-2:]
    for i, offset in enumerate(offsets):
        for low in range(2):
            start = (i * 2 + low) * GROUP
            at = pl.ds(row_offset(place, offset, low), GROUP)
            total = more[0][start : start + GROUP, :] if more else held[at, :]
            part, start = (parts[0], start) if count == 1 else (parts[i], low * GROUP)
            out[at, :] = total + part[start : start + GROUP, :]


def add_into(offsets, place, parts, mine, held, estimate):
    more = [] if mine is None else [mine]
    count = len(parts) + len(more)
    return pl.pallas_call(
        functools.partial(add_kernel, offsets, len(parts)),
        in_specs=[SMEM] + [VMEM] * (count + 1),
        out_specs=VMEM,
        out_shape=jax.ShapeDtypeStruct(held.shape, held.dtype),
        input_output_aliases={count + 1: 0},
        compiler_params=params(16),
        cost_estimate=estimate,
        name="add_into",
    )(place, *parts, *more, held)


def body(queries, slab, degree, degree_weight, spread):
    x, yh, yl, z, core = (lax.axis_index(a) for a in ("x", "yh", "yl", "z", "core"))
    columns, depth = slab.shape

    own = queries.reshape(2, CORE, GROUP, depth)
    own_other, own_mine = (
        lax.dynamic_index_in_dim(own, c, 1, keepdims=False).reshape(-1, depth) for c in (1 - core, core)
    )
    own = jnp.concatenate([own_other, own_mine])
    right_other, left_mine = shift(own_other, "x", -1), shift(own_mine, "x", 1)
    pair = shift(own, "yh", 1)

    levels = jnp.arange(degree_weight.shape[0], dtype=jnp.int32)
    one_hot_table = (degree[:, None] == levels[None, :]).astype(jnp.float32)
    weight_of = jnp.dot(one_hot_table, degree_weight, precision=lax.Precision.HIGHEST)[None, :]
    next_other, next_mine, weight_of = lax.optimization_barrier((own_other, own_mine, weight_of))
    left_other, right_mine = shift(next_other, "x", 1), shift(next_mine, "x", -1)
    weighted_slab, slab_norm = prepare(weight_of, slab)

    far_other, far_mine = shift(right_other, "x", -1), shift(left_mine, "x", 1)
    pair_left, pair_right = shift(pair, "x", 1), shift(pair, "x", -1)
    pair_far = shift(jnp.concatenate([far_other, far_mine]), "yh", 1)

    place = jnp.stack([x, yh, yl, z]).astype(jnp.int32)
    small = cost(0, 2**16)
    early_other, held = early_partial(
        EARLY,
        place,
        weight_of,
        slab_norm,
        weighted_slab,
        [own_other, pair[:KEPT], left_other, right_other, far_other]
        + [own_mine, pair[KEPT:], left_mine, right_mine, far_mine],
        cost(3 * 10**10, 2**16),
    )
    pieces = [shift(early_other, "core", 1)]
    held = add_into(EARLY, place, pieces, None, held, small)

    def partial(blocks):
        rows = jnp.concatenate(blocks)
        wide = rows.astype(jnp.float32)
        norm = jnp.sum(wide * wide * weight_of, axis=1)
        gram = lax.dot_general(
            rows, weighted_slab, (((1,), (1,)), ((), ())), preferred_element_type=jnp.float32
        )
        return norm[:, None] + slab_norm - 2.0 * gram

    late = lax.optimization_barrier((pair_far, pair_left, pair_right, early_other))[:3]
    late_other = shift(partial([b[:KEPT] for b in late]), "core", 1)
    late_mine = partial([b[KEPT:] for b in late])
    held = add_into(LATE, place, [late_other], late_mine, held, small)

    held = held.reshape(YL, Z, GROUP, columns)

    def second(k):
        return held[:, k % Z, CUT:]

    across = shift(pack(held[1, :, :CUT]), "yl", 1)
    minus = shift(pack(jnp.stack([second(-1), second(-3)])), "z", -1)
    plus = shift(pack(jnp.stack([second(1), second(3)])), "z", 1)
    opposite = shift(pack(second(4)), "z", -2)
    across, minus, plus, opposite = lax.optimization_barrier((across, minus, plus, opposite))

    def first(k):
        return held[0, k % Z, :CUT] + unpack(across[k % Z])

    second_here = second(0) + unpack(minus[0]) + unpack(plus[0])
    second_minus = second(-2) + unpack(minus[1]) + unpack(opposite)
    second_plus = second(2) + unpack(plus[1])
    across_second = shift(pack(jnp.stack([second_here[1], second_minus[1], second_plus[1]])), "yl", 1)
    minus_first = shift(pack(jnp.stack([first(-1), first(-3)])), "z", -1)
    plus_first = shift(pack(jnp.stack([first(1), first(3)])), "z", 1)
    opposite_first = shift(pack(first(4)), "z", 2)
    across_second, minus_first, plus_first, opposite_first = lax.optimization_barrier(
        (across_second, minus_first, plus_first, opposite_first)
    )

    end_minus = jnp.stack([first(-2) + unpack(minus_first[1]), second_minus[0] + unpack(across_second[1])])
    end_plus = jnp.stack(
        [first(2) + unpack(plus_first[1]) + unpack(opposite_first), second_plus[0] + unpack(across_second[2])]
    )
    end_minus, end_plus = shift(pack(end_minus), "z", -2), shift(pack(end_plus), "z", 2)
    first_sum = first(0) + unpack(minus_first[0]) + unpack(plus_first[0])
    second_sum = second_here[0] + unpack(across_second[0])
    distance = jnp.concatenate([first_sum, second_sum]) + (unpack(end_minus) + unpack(end_plus)).reshape(GROUP, columns)
    return jnp.exp(-distance / spread[0])


def solution(mesh):
    fine = Mesh(mesh.devices.reshape(X, YH, YL, Z, CORE), ("x", "yh", "yl", "z", "core"))
    placed = (P(SNAP, COEF), P(SNAP, COEF), P(COEF), P(), P())
    return jax.shard_map(
        body, mesh=fine, in_specs=placed, out_specs=P(COEF, SNAP), check_vma=False
    )
```

```python
import functools

import jax
import jax.numpy as jnp
from jax import lax
from jax.experimental import pallas as pl
from jax.experimental.pallas import tpu as pltpu
from jax.sharding import Mesh, PartitionSpec as P

X, YH, YL, Z, CORE = 4, 2, 2, 8, 2
SCALE = 2.0 ** -17
COEF = ("yl", "z", "core")
SNAP = ("x", "yh")
GROUP = 32
CUT = GROUP // 2
SPLIT = 1024
KEPT = 2 * GROUP
EARLY = ((0, 0), (0, 1), (-1, 0), (1, 0), (2, 0))
LATE = ((2, 1), (-1, 1), (1, 1))
TILE = 256
WIDE = 512
SLOTS = 4
VMEM = pl.BlockSpec(memory_space=pltpu.VMEM)
SMEM = pl.BlockSpec(memory_space=pltpu.SMEM)


def shift(value, axis, by):
    size = {"x": X, "yh": YH, "yl": YL, "z": Z, "core": CORE}[axis]
    return lax.ppermute(value, axis, [(i, (i + by) % size) for i in range(size)])


def pack(value):
    return (value * SCALE).astype(jnp.float16)


def unpack(value):
    return value.astype(jnp.float32) * (1.0 / SCALE)


def params(mib):
    return pltpu.CompilerParams(vmem_limit_bytes=mib * 2**20)


def cost(flops, moved):
    return pl.CostEstimate(flops=flops, bytes_accessed=moved, transcendentals=0)


def prepare_kernel(weight, slab, weighted, norm, parts, arrived):
    steps = slab.shape[0] // TILE

    def fetch(step):
        slot = lax.rem(step, SLOTS)
        rows = pl.ds(pl.multiple_of(step * TILE, TILE), TILE)
        return pltpu.make_async_copy(slab.at[rows, :], parts.at[slot], arrived.at[slot])

    for step in range(SLOTS):
        fetch(step).start()

    @pl.loop(0, steps)
    def _(step):
        fetch(step).wait()
        at = pl.ds(pl.multiple_of(step * TILE, TILE), TILE)
        wide = parts[lax.rem(step, SLOTS)].astype(jnp.float32)
        scaled = wide * weight[...]
        weighted[at, :] = scaled.astype(jnp.bfloat16)
        total = jnp.sum(scaled * wide, axis=1, keepdims=True)
        norm[:, at] = jnp.transpose(jnp.broadcast_to(total, (TILE, 128)))[0:1, :]

        @pl.when(step + SLOTS < steps)
        def _():
            fetch(step + SLOTS).start()


def prepare(weight, slab):
    rows, depth = slab.shape
    return pl.pallas_call(
        prepare_kernel,
        in_specs=[VMEM, pl.BlockSpec(memory_space=pltpu.HBM)],
        out_specs=[VMEM, VMEM],
        out_shape=[
            jax.ShapeDtypeStruct((rows, depth), jnp.bfloat16),
            jax.ShapeDtypeStruct((1, rows), jnp.float32),
        ],
        scratch_shapes=[
            pltpu.VMEM((SLOTS, TILE, depth), jnp.bfloat16),
            pltpu.SemaphoreType.DMA((SLOTS,)),
        ],
        compiler_params=params(44),
        cost_estimate=cost(0, 2**20),
        name="prepare",
    )(weight, slab)


def row_offset(place, offset, low):
    source_x = lax.rem(place[0] + offset[0] + X, X)
    source_yh = lax.rem(place[1] + offset[1], YH)
    yl_from_here = lax.rem(source_x // 2 + place[2], YL)
    z_to = lax.rem(source_x, 2) * 4 + source_yh * 2 + low
    z_from_here = lax.rem(z_to - place[3] + Z, Z)
    return pl.multiple_of((yl_from_here * Z + z_from_here) * GROUP, GROUP)


def early_kernel(offsets, place, weight, slab_norm, slab, *refs):
    count = len(offsets)
    blocks, (other, held, rows, norms) = refs[:-4], refs[-4:]
    blocks = (blocks[:count], blocks[count:])
    for half in range(CORE):
        for i, block in enumerate(blocks[half]):
            at = pl.ds((half * count + i) * KEPT, KEPT)
            piece = block[...]
            rows[at, :] = piece
            wide = piece.astype(jnp.float32)
            norms[at, :] = jnp.sum(wide * wide * weight[...], axis=1, keepdims=True)

    @pl.loop(0, slab.shape[0] // WIDE)
    def _(n):
        at = pl.ds(pl.multiple_of(n * WIDE, WIDE), WIDE)
        gram = lax.dot_general(
            rows[...], slab[at, :], (((1,), (1,)), ((), ())), preferred_element_type=jnp.float32
        )
        value = norms[...] + slab_norm[:, at] - 2.0 * gram
        other[:, at] = value[: count * KEPT]
        for i, offset in enumerate(offsets):
            for low in range(2):
                start = (count + i) * KEPT + low * GROUP
                held[pl.ds(row_offset(place, offset, low), GROUP), at] = value[start : start + GROUP]


def early_partial(offsets, place, weight, slab_norm, slab, blocks, estimate):
    columns, depth = slab.shape
    kept = len(offsets) * KEPT
    arguments = [place, weight, slab_norm, slab, *blocks]
    return pl.pallas_call(
        functools.partial(early_kernel, offsets),
        in_specs=[SMEM] + [VMEM] * (len(arguments) - 1),
        out_specs=[VMEM, VMEM],
        out_shape=[
            jax.ShapeDtypeStruct((kept, columns), jnp.float32),
            jax.ShapeDtypeStruct((YL * Z * GROUP, columns), jnp.float32),
        ],
        scratch_shapes=[
            pltpu.VMEM((kept * CORE, depth), jnp.bfloat16),
            pltpu.VMEM((kept * CORE, 1), jnp.float32),
        ],
        compiler_params=params(24),
        cost_estimate=estimate,
        name="early_partial",
    )(*arguments)


def add_kernel(offsets, count, place, *refs):
    parts, more, (held, out) = refs[:count], refs[count:-2], refs[-2:]
    for i, offset in enumerate(offsets):
        for low in range(2):
            start = (i * 2 + low) * GROUP
            at = pl.ds(row_offset(place, offset, low), GROUP)
            total = more[0][start : start + GROUP, :] if more else held[at, :]
            part, start = (parts[0], start) if count == 1 else (parts[i], low * GROUP)
            out[at, :] = total + part[start : start + GROUP, :]


def add_into(offsets, place, parts, mine, held, estimate):
    more = [] if mine is None else [mine]
    count = len(parts) + len(more)
    return pl.pallas_call(
        functools.partial(add_kernel, offsets, len(parts)),
        in_specs=[SMEM] + [VMEM] * (count + 1),
        out_specs=VMEM,
        out_shape=jax.ShapeDtypeStruct(held.shape, held.dtype),
        input_output_aliases={count + 1: 0},
        compiler_params=params(16),
        cost_estimate=estimate,
        name="add_into",
    )(place, *parts, *more, held)


def body(queries, slab, degree, degree_weight, spread):
    x, yh, yl, z, core = (lax.axis_index(a) for a in ("x", "yh", "yl", "z", "core"))
    columns, depth = slab.shape

    own = queries.reshape(2, CORE, GROUP, depth)
    own_other, own_mine = (
        lax.dynamic_index_in_dim(own, c, 1, keepdims=False).reshape(-1, depth) for c in (1 - core, core)
    )
    own = jnp.concatenate([own_other, own_mine])
    right_other, left_mine = shift(own_other, "x", -1), shift(own_mine, "x", 1)
    pair = shift(own, "yh", 1)

    levels = jnp.arange(degree_weight.shape[0], dtype=jnp.int32)
    one_hot_table = (degree[:, None] == levels[None, :]).astype(jnp.float32)
    weight_of = jnp.dot(one_hot_table, degree_weight, precision=lax.Precision.HIGHEST)[None, :]
    next_other, next_mine, weight_of = lax.optimization_barrier((own_other, own_mine, weight_of))
    left_other, right_mine = shift(next_other, "x", 1), shift(next_mine, "x", -1)
    weighted_slab, slab_norm = prepare(weight_of, slab)

    far_other, far_mine = shift(right_other, "x", -1), shift(left_mine, "x", 1)
    pair_left, pair_right = shift(pair, "x", 1), shift(pair, "x", -1)
    pair_far = shift(jnp.concatenate([far_other, far_mine]), "yh", 1)

    place = jnp.stack([x, yh, yl, z]).astype(jnp.int32)
    small = cost(0, 2**16)
    early_other, held = early_partial(
        EARLY,
        place,
        weight_of,
        slab_norm,
        weighted_slab,
        [own_other, pair[:KEPT], left_other, right_other, far_other]
        + [own_mine, pair[KEPT:], left_mine, right_mine, far_mine],
        cost(3 * 10**10, 2**16),
    )
    pieces = [shift(early_other, "core", 1)]
    held = add_into(EARLY, place, pieces, None, held, small)

    def partial(blocks):
        rows = jnp.concatenate(blocks)
        wide = rows.astype(jnp.float32)
        norm = jnp.sum(wide * wide * weight_of, axis=1)
        gram = lax.dot_general(
            rows, weighted_slab, (((1,), (1,)), ((), ())), preferred_element_type=jnp.float32
        )
        return norm[:, None] + slab_norm - 2.0 * gram

    late = lax.optimization_barrier((pair_far, pair_left, pair_right, early_other))[:3]
    late_other = shift(partial([b[:KEPT] for b in late]), "core", 1)
    late_mine = partial([b[KEPT:] for b in late])
    held = add_into(LATE, place, [late_other], late_mine, held, small)

    held = held.reshape(YL, Z, GROUP, columns)

    def second(k):
        return held[:, k % Z, :, SPLIT:]

    across = shift(pack(held[1, :, :, :SPLIT]), "yl", 1)
    plus = shift(pack(jnp.stack([second(1), second(3)])), "z", 1)
    minus = shift(pack(jnp.stack([second(-1), second(-3)])), "z", -1)
    far_plus = shift(pack(second(4)[:, CUT:]), "z", 2)
    far_minus = shift(pack(second(4)[:, :CUT]), "z", -2)
    across, plus, minus, far_plus, far_minus = lax.optimization_barrier((across, plus, minus, far_plus, far_minus))

    def first(k):
        return held[0, k % Z, :, :SPLIT] + unpack(across[k % Z])

    second_here = second(0) + unpack(minus[0]) + unpack(plus[0])
    top, bottom = ((0, 0), (0, CUT), (0, 0)), ((0, 0), (CUT, 0), (0, 0))
    second_minus = second(-2) + unpack(minus[1]) + jnp.pad(unpack(far_minus), top)
    second_plus = second(2) + unpack(plus[1]) + jnp.pad(unpack(far_plus), bottom)
    across_second = shift(pack(jnp.stack([second_here[1], second_minus[1], second_plus[1]])), "yl", 1)
    plus_first = shift(pack(jnp.stack([first(1), first(3)])), "z", 1)
    minus_first = shift(pack(jnp.stack([first(-1), first(-3)])), "z", -1)
    opposite_first = shift(pack(first(4)), "z", 2)
    across_second, plus_first, minus_first, opposite_first = lax.optimization_barrier(
        (across_second, plus_first, minus_first, opposite_first)
    )

    end_minus = jnp.concatenate(
        [first(-2) + unpack(minus_first[1]), second_minus[0] + unpack(across_second[1])], axis=1
    )
    end_plus = jnp.concatenate(
        [first(2) + unpack(plus_first[1]) + unpack(opposite_first), second_plus[0] + unpack(across_second[2])], axis=1
    )
    end_plus, end_minus = shift(pack(end_plus), "z", 2), shift(pack(end_minus), "z", -2)
    first_sum = first(0) + unpack(minus_first[0]) + unpack(plus_first[0])
    second_sum = second_here[0] + unpack(across_second[0])
    distance = jnp.concatenate([first_sum, second_sum], axis=1) + unpack(end_minus) + unpack(end_plus)
    return jnp.exp(-distance / spread[0])


def solution(mesh):
    fine = Mesh(mesh.devices.reshape(X, YH, YL, Z, CORE), ("x", "yh", "yl", "z", "core"))
    placed = (P(SNAP, COEF), P(SNAP, COEF), P(COEF), P(), P())
    return jax.shard_map(
        body, mesh=fine, in_specs=placed, out_specs=P(COEF, SNAP), check_vma=False
    )
```

```python
import functools

import jax
import jax.numpy as jnp
from jax import lax
from jax.experimental import pallas as pl
from jax.experimental.pallas import tpu as pltpu
from jax.sharding import Mesh, PartitionSpec as P

X, YH, YL, Z, CORE = 4, 2, 2, 8, 2
SCALE = 2.0 ** -17
COEF = ("yl", "z", "core")
SNAP = ("x", "yh")
GROUP = 32
CUT = GROUP // 2
SPLIT = 1024
KEPT = 2 * GROUP
EARLY = ((0, 0), (0, 1), (-1, 0), (1, 0), (2, 0))
LATE = ((2, 1), (-1, 1), (1, 1))
TILE = 256
WIDE = 512
SLOTS = 4
VMEM = pl.BlockSpec(memory_space=pltpu.VMEM)
SMEM = pl.BlockSpec(memory_space=pltpu.SMEM)


def shift(value, axis, by):
    size = {"x": X, "yh": YH, "yl": YL, "z": Z, "core": CORE}[axis]
    return lax.ppermute(value, axis, [(i, (i + by) % size) for i in range(size)])


def pack(value):
    return (value * SCALE).astype(jnp.float16)


def unpack(value):
    return value.astype(jnp.float32) * (1.0 / SCALE)


def params(mib):
    return pltpu.CompilerParams(vmem_limit_bytes=mib * 2**20)


def cost(flops, moved):
    return pl.CostEstimate(flops=flops, bytes_accessed=moved, transcendentals=0)


def prepare_kernel(weight, slab, weighted, norm, parts, arrived):
    steps = slab.shape[0] // TILE

    def fetch(step):
        slot = lax.rem(step, SLOTS)
        rows = pl.ds(pl.multiple_of(step * TILE, TILE), TILE)
        return pltpu.make_async_copy(slab.at[rows, :], parts.at[slot], arrived.at[slot])

    for step in range(SLOTS):
        fetch(step).start()

    @pl.loop(0, steps)
    def _(step):
        fetch(step).wait()
        at = pl.ds(pl.multiple_of(step * TILE, TILE), TILE)
        wide = parts[lax.rem(step, SLOTS)].astype(jnp.float32)
        scaled = wide * weight[...]
        weighted[at, :] = scaled.astype(jnp.bfloat16)
        total = jnp.sum(scaled * wide, axis=1, keepdims=True)
        norm[:, at] = jnp.transpose(jnp.broadcast_to(total, (TILE, 128)))[0:1, :]

        @pl.when(step + SLOTS < steps)
        def _():
            fetch(step + SLOTS).start()


def prepare(weight, slab):
    rows, depth = slab.shape
    return pl.pallas_call(
        prepare_kernel,
        in_specs=[VMEM, pl.BlockSpec(memory_space=pltpu.HBM)],
        out_specs=[VMEM, VMEM],
        out_shape=[
            jax.ShapeDtypeStruct((rows, depth), jnp.bfloat16),
            jax.ShapeDtypeStruct((1, rows), jnp.float32),
        ],
        scratch_shapes=[
            pltpu.VMEM((SLOTS, TILE, depth), jnp.bfloat16),
            pltpu.SemaphoreType.DMA((SLOTS,)),
        ],
        compiler_params=params(44),
        cost_estimate=cost(10**10, 2**20),
        name="prepare",
    )(weight, slab)


def row_offset(place, offset, low):
    source_x = lax.rem(place[0] + offset[0] + X, X)
    source_yh = lax.rem(place[1] + offset[1], YH)
    yl_from_here = lax.rem(source_x // 2 + place[2], YL)
    z_to = lax.rem(source_x, 2) * 4 + source_yh * 2 + low
    z_from_here = lax.rem(z_to - place[3] + Z, Z)
    return pl.multiple_of((yl_from_here * Z + z_from_here) * GROUP, GROUP)


def early_kernel(offsets, place, weight, slab_norm, slab, *refs):
    count = len(offsets)
    blocks, (other, held, rows, norms) = refs[:-4], refs[-4:]
    blocks = (blocks[:count], blocks[count:])
    for half in range(CORE):
        for i, block in enumerate(blocks[half]):
            at = pl.ds((half * count + i) * KEPT, KEPT)
            piece = block[...]
            rows[at, :] = piece
            wide = piece.astype(jnp.float32)
            norms[at, :] = jnp.sum(wide * wide * weight[...], axis=1, keepdims=True)

    @pl.loop(0, slab.shape[0] // WIDE)
    def _(n):
        at = pl.ds(pl.multiple_of(n * WIDE, WIDE), WIDE)
        gram = lax.dot_general(
            rows[...], slab[at, :], (((1,), (1,)), ((), ())), preferred_element_type=jnp.float32
        )
        value = norms[...] + slab_norm[:, at] - 2.0 * gram
        other[:, at] = value[: count * KEPT]
        for i, offset in enumerate(offsets):
            for low in range(2):
                start = (count + i) * KEPT + low * GROUP
                held[pl.ds(row_offset(place, offset, low), GROUP), at] = value[start : start + GROUP]


def early_partial(offsets, place, weight, slab_norm, slab, blocks, estimate):
    columns, depth = slab.shape
    kept = len(offsets) * KEPT
    arguments = [place, weight, slab_norm, slab, *blocks]
    return pl.pallas_call(
        functools.partial(early_kernel, offsets),
        in_specs=[SMEM] + [VMEM] * (len(arguments) - 1),
        out_specs=[VMEM, VMEM],
        out_shape=[
            jax.ShapeDtypeStruct((kept, columns), jnp.float32),
            jax.ShapeDtypeStruct((YL * Z * GROUP, columns), jnp.float32),
        ],
        scratch_shapes=[
            pltpu.VMEM((kept * CORE, depth), jnp.bfloat16),
            pltpu.VMEM((kept * CORE, 1), jnp.float32),
        ],
        compiler_params=params(24),
        cost_estimate=estimate,
        name="early_partial",
    )(*arguments)


def add_kernel(offsets, count, place, *refs):
    parts, more, (held, out) = refs[:count], refs[count:-2], refs[-2:]
    for i, offset in enumerate(offsets):
        for low in range(2):
            start = (i * 2 + low) * GROUP
            at = pl.ds(row_offset(place, offset, low), GROUP)
            total = more[0][start : start + GROUP, :] if more else held[at, :]
            part, start = (parts[0], start) if count == 1 else (parts[i], low * GROUP)
            out[at, :] = total + part[start : start + GROUP, :]


def add_into(offsets, place, parts, mine, held, estimate):
    more = [] if mine is None else [mine]
    count = len(parts) + len(more)
    return pl.pallas_call(
        functools.partial(add_kernel, offsets, len(parts)),
        in_specs=[SMEM] + [VMEM] * (count + 1),
        out_specs=VMEM,
        out_shape=jax.ShapeDtypeStruct(held.shape, held.dtype),
        input_output_aliases={count + 1: 0},
        compiler_params=params(16),
        cost_estimate=estimate,
        name="add_into",
    )(place, *parts, *more, held)


def body(queries, slab, degree, degree_weight, spread):
    x, yh, yl, z, core = (lax.axis_index(a) for a in ("x", "yh", "yl", "z", "core"))
    columns, depth = slab.shape

    own = queries.reshape(2, CORE, GROUP, depth)
    own_other, own_mine = (
        lax.dynamic_index_in_dim(own, c, 1, keepdims=False).reshape(-1, depth) for c in (1 - core, core)
    )
    own = jnp.concatenate([own_other, own_mine])
    right_other, left_mine = shift(own_other, "x", -1), shift(own_mine, "x", 1)
    pair = shift(own, "yh", 1)

    levels = jnp.arange(degree_weight.shape[0], dtype=jnp.int32)
    one_hot_table = (degree[:, None] == levels[None, :]).astype(jnp.float32)
    weight_of = jnp.dot(one_hot_table, degree_weight, precision=lax.Precision.HIGHEST)[None, :]
    next_other, next_mine, weight_of = lax.optimization_barrier((own_other, own_mine, weight_of))
    left_other, right_mine = shift(next_other, "x", 1), shift(next_mine, "x", -1)
    weight_of, pair = lax.optimization_barrier((weight_of, pair))
    weighted_slab, slab_norm = prepare(weight_of, slab)

    far_other, far_mine = shift(right_other, "x", -1), shift(left_mine, "x", 1)
    pair_left, pair_right = shift(pair, "x", 1), shift(pair, "x", -1)
    pair_far = shift(jnp.concatenate([far_other, far_mine]), "yh", 1)

    place = jnp.stack([x, yh, yl, z]).astype(jnp.int32)
    small = cost(0, 2**16)
    early_other, held = early_partial(
        EARLY,
        place,
        weight_of,
        slab_norm,
        weighted_slab,
        [own_other, pair[:KEPT], left_other, right_other, far_other]
        + [own_mine, pair[KEPT:], left_mine, right_mine, far_mine],
        cost(3 * 10**10, 2**16),
    )
    pieces = [shift(early_other, "core", 1)]
    held = add_into(EARLY, place, pieces, None, held, small)

    def partial(blocks):
        rows = jnp.concatenate(blocks)
        wide = rows.astype(jnp.float32)
        norm = jnp.sum(wide * wide * weight_of, axis=1)
        gram = lax.dot_general(
            rows, weighted_slab, (((1,), (1,)), ((), ())), preferred_element_type=jnp.float32
        )
        return norm[:, None] + slab_norm - 2.0 * gram

    late = lax.optimization_barrier((pair_far, pair_left, pair_right, early_other))[:3]
    late_other = shift(partial([b[:KEPT] for b in late]), "core", 1)
    late_mine = partial([b[KEPT:] for b in late])
    held = add_into(LATE, place, [late_other], late_mine, held, small)

    held = held.reshape(YL, Z, GROUP, columns)

    def second(k):
        return held[:, k % Z, :, SPLIT:]

    across = shift(pack(held[1, :, :, :SPLIT]), "yl", 1)
    plus = shift(pack(jnp.stack([second(1), second(3)])), "z", 1)
    minus = shift(pack(jnp.stack([second(-1), second(-3)])), "z", -1)
    far_plus = shift(pack(second(4)[:, CUT:]), "z", 2)
    far_minus = shift(pack(second(4)[:, :CUT]), "z", -2)
    across, plus, minus, far_plus, far_minus = lax.optimization_barrier((across, plus, minus, far_plus, far_minus))

    def first(k):
        return held[0, k % Z, :, :SPLIT] + unpack(across[k % Z])

    second_here = second(0) + unpack(minus[0]) + unpack(plus[0])
    top, bottom = ((0, 0), (0, CUT), (0, 0)), ((0, 0), (CUT, 0), (0, 0))
    second_minus = second(-2) + unpack(minus[1]) + jnp.pad(unpack(far_minus), top)
    second_plus = second(2) + unpack(plus[1]) + jnp.pad(unpack(far_plus), bottom)
    across_second = shift(pack(jnp.stack([second_here[1], second_minus[1], second_plus[1]])), "yl", 1)
    plus_first = shift(pack(jnp.stack([first(1), first(3)])), "z", 1)
    minus_first = shift(pack(jnp.stack([first(-1), first(-3)])), "z", -1)
    opposite_first = shift(pack(first(4)), "z", 2)
    across_second, plus_first, minus_first, opposite_first = lax.optimization_barrier(
        (across_second, plus_first, minus_first, opposite_first)
    )

    end_minus = jnp.concatenate(
        [first(-2) + unpack(minus_first[1]), second_minus[0] + unpack(across_second[1])], axis=1
    )
    end_plus = jnp.concatenate(
        [first(2) + unpack(plus_first[1]) + unpack(opposite_first), second_plus[0] + unpack(across_second[2])], axis=1
    )
    end_plus, end_minus = shift(pack(end_plus), "z", 2), shift(pack(end_minus), "z", -2)
    first_sum = first(0) + unpack(minus_first[0]) + unpack(plus_first[0])
    second_sum = second_here[0] + unpack(across_second[0])
    distance = jnp.concatenate([first_sum, second_sum], axis=1) + unpack(end_minus) + unpack(end_plus)
    return jnp.exp(-distance / spread[0])


def solution(mesh):
    fine = Mesh(mesh.devices.reshape(X, YH, YL, Z, CORE), ("x", "yh", "yl", "z", "core"))
    placed = (P(SNAP, COEF), P(SNAP, COEF), P(COEF), P(), P())
    return jax.shard_map(
        body, mesh=fine, in_specs=placed, out_specs=P(COEF, SNAP), check_vma=False
    )
```

```python
import functools

import jax
import jax.numpy as jnp
from jax import lax
from jax.experimental import pallas as pl
from jax.experimental.pallas import tpu as pltpu
from jax.sharding import Mesh, PartitionSpec as P

X, YH, YL, Z, CORE = 4, 2, 2, 8, 2
SCALE = 2.0 ** -17
COEF = ("yl", "z", "core")
SNAP = ("x", "yh")
GROUP = 32
CUT = GROUP // 2
SPLIT = 1024
KEPT = 2 * GROUP
EARLY = ((0, 0), (0, 1), (-1, 0), (1, 0), (2, 0))
LATE = ((2, 1), (-1, 1), (1, 1))
TILE = 256
WIDE = 512
SLOTS = 4
VMEM = pl.BlockSpec(memory_space=pltpu.VMEM)
SMEM = pl.BlockSpec(memory_space=pltpu.SMEM)


def shift(value, axis, by):
    size = {"x": X, "yh": YH, "yl": YL, "z": Z, "core": CORE}[axis]
    return lax.ppermute(value, axis, [(i, (i + by) % size) for i in range(size)])


def pack(value):
    return (value * SCALE).astype(jnp.float16)


def unpack(value):
    return value.astype(jnp.float32) * (1.0 / SCALE)


def params(mib):
    return pltpu.CompilerParams(vmem_limit_bytes=mib * 2**20)


def cost(flops, moved):
    return pl.CostEstimate(flops=flops, bytes_accessed=moved, transcendentals=0)


def prepare_kernel(weight, slab, weighted, norm, parts, arrived):
    steps = slab.shape[0] // TILE

    def fetch(step):
        slot = lax.rem(step, SLOTS)
        rows = pl.ds(pl.multiple_of(step * TILE, TILE), TILE)
        return pltpu.make_async_copy(slab.at[rows, :], parts.at[slot], arrived.at[slot])

    for step in range(SLOTS):
        fetch(step).start()

    @pl.loop(0, steps)
    def _(step):
        fetch(step).wait()
        at = pl.ds(pl.multiple_of(step * TILE, TILE), TILE)
        wide = parts[lax.rem(step, SLOTS)].astype(jnp.float32)
        scaled = wide * weight[...]
        weighted[at, :] = scaled.astype(jnp.bfloat16)
        total = jnp.sum(scaled * wide, axis=1, keepdims=True)
        norm[:, at] = jnp.transpose(jnp.broadcast_to(total, (TILE, 128)))[0:1, :]

        @pl.when(step + SLOTS < steps)
        def _():
            fetch(step + SLOTS).start()


def prepare(weight, slab):
    rows, depth = slab.shape
    return pl.pallas_call(
        prepare_kernel,
        in_specs=[VMEM, pl.BlockSpec(memory_space=pltpu.HBM)],
        out_specs=[VMEM, VMEM],
        out_shape=[
            jax.ShapeDtypeStruct((rows, depth), jnp.bfloat16),
            jax.ShapeDtypeStruct((1, rows), jnp.float32),
        ],
        scratch_shapes=[
            pltpu.VMEM((SLOTS, TILE, depth), jnp.bfloat16),
            pltpu.SemaphoreType.DMA((SLOTS,)),
        ],
        compiler_params=params(44),
        cost_estimate=cost(10**10, 2**20),
        name="prepare",
    )(weight, slab)


def row_offset(place, offset, low):
    source_x = lax.rem(place[0] + offset[0] + X, X)
    source_yh = lax.rem(place[1] + offset[1], YH)
    yl_from_here = lax.rem(source_x // 2 + place[2], YL)
    z_to = lax.rem(source_x, 2) * 4 + source_yh * 2 + low
    z_from_here = lax.rem(z_to - place[3] + Z, Z)
    return pl.multiple_of((yl_from_here * Z + z_from_here) * GROUP, GROUP)


def early_kernel(offsets, place, weight, slab_norm, slab, *refs):
    count = len(offsets)
    blocks, (other, held, rows, norms) = refs[:-4], refs[-4:]
    blocks = (blocks[:count], blocks[count:])
    for half in range(CORE):
        for i, block in enumerate(blocks[half]):
            at = pl.ds((half * count + i) * KEPT, KEPT)
            piece = block[...]
            rows[at, :] = piece
            wide = piece.astype(jnp.float32)
            norms[at, :] = jnp.sum(wide * wide * weight[...], axis=1, keepdims=True)

    @pl.loop(0, slab.shape[0] // WIDE)
    def _(n):
        at = pl.ds(pl.multiple_of(n * WIDE, WIDE), WIDE)
        gram = lax.dot_general(
            rows[...], slab[at, :], (((1,), (1,)), ((), ())), preferred_element_type=jnp.float32
        )
        value = norms[...] + slab_norm[:, at] - 2.0 * gram
        other[:, at] = value[: count * KEPT]
        for i, offset in enumerate(offsets):
            for low in range(2):
                start = (count + i) * KEPT + low * GROUP
                held[pl.ds(row_offset(place, offset, low), GROUP), at] = value[start : start + GROUP]


def early_partial(offsets, place, weight, slab_norm, slab, blocks, estimate):
    columns, depth = slab.shape
    kept = len(offsets) * KEPT
    arguments = [place, weight, slab_norm, slab, *blocks]
    return pl.pallas_call(
        functools.partial(early_kernel, offsets),
        in_specs=[SMEM] + [VMEM] * (len(arguments) - 1),
        out_specs=[VMEM, VMEM],
        out_shape=[
            jax.ShapeDtypeStruct((kept, columns), jnp.float32),
            jax.ShapeDtypeStruct((YL * Z * GROUP, columns), jnp.float32),
        ],
        scratch_shapes=[
            pltpu.VMEM((kept * CORE, depth), jnp.bfloat16),
            pltpu.VMEM((kept * CORE, 1), jnp.float32),
        ],
        compiler_params=params(24),
        cost_estimate=estimate,
        name="early_partial",
    )(*arguments)


def add_kernel(groups, place, *refs):
    refs, (held, out) = list(refs[:-2]), refs[-2:]
    for offsets, has_mine in groups:
        received = refs.pop(0)
        mine = refs.pop(0) if has_mine else None
        for i, offset in enumerate(offsets):
            for low in range(2):
                start = (i * 2 + low) * GROUP
                at = pl.ds(row_offset(place, offset, low), GROUP)
                total = held[at, :] if mine is None else mine[start : start + GROUP, :]
                out[at, :] = total + received[start : start + GROUP, :]


def add_into(groups, place, held, estimate):
    parts = [p for _, received, mine in groups for p in (received, mine) if p is not None]
    return pl.pallas_call(
        functools.partial(add_kernel, [(offsets, mine is not None) for offsets, _, mine in groups]),
        in_specs=[SMEM] + [VMEM] * (len(parts) + 1),
        out_specs=VMEM,
        out_shape=jax.ShapeDtypeStruct(held.shape, held.dtype),
        input_output_aliases={len(parts) + 1: 0},
        compiler_params=params(20),
        cost_estimate=estimate,
        name="add_into",
    )(place, *parts, held)


def body(queries, slab, degree, degree_weight, spread):
    x, yh, yl, z, core = (lax.axis_index(a) for a in ("x", "yh", "yl", "z", "core"))
    columns, depth = slab.shape

    own = queries.reshape(2, CORE, GROUP, depth)
    own_other, own_mine = (
        lax.dynamic_index_in_dim(own, c, 1, keepdims=False).reshape(-1, depth) for c in (1 - core, core)
    )
    own = jnp.concatenate([own_other, own_mine])
    right_other, left_mine = shift(own_other, "x", -1), shift(own_mine, "x", 1)
    pair = shift(own, "yh", 1)

    levels = jnp.arange(degree_weight.shape[0], dtype=jnp.int32)
    one_hot_table = (degree[:, None] == levels[None, :]).astype(jnp.float32)
    weight_of = jnp.dot(one_hot_table, degree_weight, precision=lax.Precision.HIGHEST)[None, :]
    next_other, next_mine, weight_of = lax.optimization_barrier((own_other, own_mine, weight_of))
    left_other, right_mine = shift(next_other, "x", 1), shift(next_mine, "x", -1)

    weight_of, pair = lax.optimization_barrier((weight_of, pair))
    weighted_slab, slab_norm = prepare(weight_of, slab)

    far_other, far_mine = shift(right_other, "x", -1), shift(left_mine, "x", 1)
    pair_left, pair_right = shift(pair, "x", 1), shift(pair, "x", -1)
    pair_far = shift(jnp.concatenate([far_other, far_mine]), "yh", 1)

    place = jnp.stack([x, yh, yl, z]).astype(jnp.int32)
    small = cost(0, 2**16)
    early_other, held = early_partial(
        EARLY,
        place,
        weight_of,
        slab_norm,
        weighted_slab,
        [own_other, pair[:KEPT], left_other, right_other, far_other]
        + [own_mine, pair[KEPT:], left_mine, right_mine, far_mine],
        cost(3 * 10**10, 2**16),
    )
    early = EARLY, shift(early_other, "core", 1), None

    def partial(blocks):
        rows = jnp.concatenate(blocks)
        wide = rows.astype(jnp.float32)
        norm = jnp.sum(wide * wide * weight_of, axis=1)
        gram = lax.dot_general(
            rows, weighted_slab, (((1,), (1,)), ((), ())), preferred_element_type=jnp.float32
        )
        return norm[:, None] + slab_norm - 2.0 * gram

    late = lax.optimization_barrier((pair_far, pair_left, pair_right, early_other))[:3]
    late_other = shift(partial([b[:KEPT] for b in late]), "core", 1)
    late_mine = partial([b[KEPT:] for b in late])
    held = add_into([early, (LATE, late_other, late_mine)], place, held, small)

    held = held.reshape(YL, Z, GROUP, columns)

    def second(k):
        return held[:, k % Z, :, SPLIT:]

    across = shift(pack(held[1, :, :, :SPLIT]), "yl", 1)
    plus = shift(pack(jnp.stack([second(1), second(3)])), "z", 1)
    minus = shift(pack(jnp.stack([second(-1), second(-3)])), "z", -1)
    far_plus = shift(pack(second(4)[:, CUT:]), "z", 2)
    far_minus = shift(pack(second(4)[:, :CUT]), "z", -2)
    across, plus, minus, far_plus, far_minus = lax.optimization_barrier((across, plus, minus, far_plus, far_minus))

    def first(k):
        return held[0, k % Z, :, :SPLIT] + unpack(across[k % Z])

    second_here = second(0) + unpack(minus[0]) + unpack(plus[0])
    top, bottom = ((0, 0), (0, CUT), (0, 0)), ((0, 0), (CUT, 0), (0, 0))
    second_minus = second(-2) + unpack(minus[1]) + jnp.pad(unpack(far_minus), top)
    second_plus = second(2) + unpack(plus[1]) + jnp.pad(unpack(far_plus), bottom)
    across_second = shift(pack(jnp.stack([second_here[1], second_minus[1], second_plus[1]])), "yl", 1)
    plus_first = shift(pack(jnp.stack([first(1), first(3)])), "z", 1)
    minus_first = shift(pack(jnp.stack([first(-1), first(-3)])), "z", -1)
    opposite_first = shift(pack(first(4)), "z", 2)
    across_second, plus_first, minus_first, opposite_first = lax.optimization_barrier(
        (across_second, plus_first, minus_first, opposite_first)
    )

    end_minus = jnp.concatenate(
        [first(-2) + unpack(minus_first[1]), second_minus[0] + unpack(across_second[1])], axis=1
    )
    end_plus = jnp.concatenate(
        [first(2) + unpack(plus_first[1]) + unpack(opposite_first), second_plus[0] + unpack(across_second[2])], axis=1
    )
    end_plus, end_minus = shift(pack(end_plus), "z", 2), shift(pack(end_minus), "z", -2)
    first_sum = first(0) + unpack(minus_first[0]) + unpack(plus_first[0])
    second_sum = second_here[0] + unpack(across_second[0])
    distance = jnp.concatenate([first_sum, second_sum], axis=1) + unpack(end_minus) + unpack(end_plus)
    return jnp.exp(-distance / spread[0])


def solution(mesh):
    fine = Mesh(mesh.devices.reshape(X, YH, YL, Z, CORE), ("x", "yh", "yl", "z", "core"))
    placed = (P(SNAP, COEF), P(SNAP, COEF), P(COEF), P(), P())
    return jax.shard_map(
        body, mesh=fine, in_specs=placed, out_specs=P(COEF, SNAP), check_vma=False
    )
```
